32 devices in a mesh: row: 4 (over x, core), col: 8 (over z, y).
Axes of the slice: x: 2, y: 2, z: 4, core: 2. Of those that a mesh axis runs over, the one named last changes fastest.
Arguments:
- features: bfloat16 [32768, 256], P(('row', 'col')), may hold values from -6 to 6
- weight: bfloat16 [256, 256], replicated, may hold values from -0.375 to 0.375
- layer_bias: float32 [256], replicated, may hold values from -3 to 3
- adj_tiles: bfloat16 [1536, 128, 128], P(('row', 'col')), may hold values from 0 to 0.079589844
- tile_source: int32 [1536], P(('row', 'col')), may hold values from 0 to 11, as said below
- tile_target: int32 [1536], P(('row', 'col')), may hold values from 0 to 23, as said below
- tile_count: int32 [32], P(('row', 'col')), may hold values from 1 to 48, as said below
- fetch_list: int32 [128, 3], P(('row', 'col')), may hold values from -1 to 7, as said below
- deliver_list: int32 [256, 3], P(('row', 'col')), may hold values from -1 to 7, as said below
- cotangent: bfloat16 [32768, 256], P(('row', 'col')), may hold values from -6 to 6
Outputs:
- layer_out: bfloat16 [32768, 256], P(('row', 'col'))
- grad_features: bfloat16 [32768, 256], P(('row', 'col'))
- grad_weight: float32 [256, 256], replicated
- grad_bias: float32 [256], replicated
The draws below stay inside these ranges and needn't reach their ends.
Inputs may be any that keep to these rules, and one draw needn't show every extreme that they name: `tile_source`: each entry names a source slot q * 3 + j of its device whose fetch_list entry is not -1. `tile_target`: each entry names a row slot p * 3 + j of its device whose deliver_list entry is not -1. `tile_count`: live tiles are the first ones of a device; in every draw some device has 48 live tiles. `fetch_list`: each list holds one or more distinct local block numbers, then -1 in its unused slots; in every draw some device has all its lists full. `deliver_list`: each list holds one or more distinct local block numbers, then -1 in its unused slots; in every draw some owner has all its lists full.
All inputs are finite; a program needn't handle non-finite values.
Results may differ from the reference program's by a relative error of at most 0.0085.
Values may be sent and summed in bfloat16 or wider, within the bound.
A program may use at most 128 MiB of HBM per device.

```python
import jax
import jax.numpy as jnp
from jax import lax

F = 256
TILE = 128
BLK_DEV = 8
TILES_DEV = 48
CAPF = 3
CAPO = 3
GRID_ROWS = 4
GRID_COLS = 8
MESH_DEVICES = 32
NODES = 32768
SRC_SLOTS = 12
ROW_SLOTS = 24


def distinct_blocks(lists_key, rows_total, capacity):
    scores = jax.random.randint(lists_key, (rows_total, BLK_DEV), 0, 1 << 20)
    scores = scores * BLK_DEV + jnp.arange(BLK_DEV, dtype=jnp.int32)[None, :]
    ranking = jnp.argsort(scores, axis=1, stable=True)
    return ranking[:, :capacity].astype(jnp.int32)


def fetch_tables(key):
    lists_key = jax.random.fold_in(key, 11)
    rows_total = MESH_DEVICES * GRID_ROWS
    lengths = jax.random.randint(jax.random.fold_in(lists_key, 1), (rows_total,), 1, CAPF + 1)
    chosen = jax.random.randint(jax.random.fold_in(lists_key, 2), (), 0, MESH_DEVICES)
    row_owner = jnp.arange(rows_total, dtype=jnp.int32) // GRID_ROWS
    lengths = jnp.where(row_owner == chosen, CAPF, lengths).astype(jnp.int32)
    entries = distinct_blocks(jax.random.fold_in(lists_key, 3), rows_total, CAPF)
    listing = jnp.where(jnp.arange(CAPF, dtype=jnp.int32)[None, :] < lengths[:, None], entries, -1)
    return (listing.astype(jnp.int32), lengths, chosen)


def deliver_tables(key):
    lists_key = jax.random.fold_in(key, 12)
    rows_total = MESH_DEVICES * GRID_COLS
    lengths = jax.random.randint(jax.random.fold_in(lists_key, 1), (rows_total,), 1, CAPO + 1)
    chosen_row = jax.random.randint(jax.random.fold_in(lists_key, 2), (), 0, GRID_ROWS)
    chosen = chosen_row * GRID_COLS + GRID_COLS - 1
    row_owner = jnp.arange(rows_total, dtype=jnp.int32) // GRID_COLS
    lengths = jnp.where(row_owner == chosen, CAPO, lengths).astype(jnp.int32)
    entries = distinct_blocks(jax.random.fold_in(lists_key, 3), rows_total, CAPO)
    listing = jnp.where(jnp.arange(CAPO, dtype=jnp.int32)[None, :] < lengths[:, None], entries, -1)
    return (listing.astype(jnp.int32), lengths, chosen_row)


def draw_fetch_list(key, part):
    tables = fetch_tables(key)
    return tables[0]


def draw_deliver_list(key, part):
    tables = deliver_tables(key)
    return tables[0]


def draw_tile_source(key, part):
    tables = fetch_tables(key)
    lengths = tables[1]
    chosen = tables[2]
    device_ids = jnp.arange(MESH_DEVICES, dtype=jnp.int32)[:, None]
    owners = jax.random.randint(jax.random.fold_in(key, 21), (MESH_DEVICES, TILES_DEV), 0, GRID_ROWS)
    raw_bits = jax.random.randint(jax.random.fold_in(key, 22), (MESH_DEVICES, TILES_DEV), 0, 1 << 20)
    available = lengths[device_ids * GRID_ROWS + owners]
    slots = owners * CAPF + raw_bits % available
    positions = jnp.arange(TILES_DEV, dtype=jnp.int32)[None, :]
    slots = jnp.where((device_ids == chosen) & (positions == 0), SRC_SLOTS - 1, slots)
    slots = jnp.where((device_ids == chosen) & (positions == 1), 0, slots)
    return slots.reshape(-1).astype(jnp.int32)


def draw_tile_target(key, part):
    tables = deliver_tables(key)
    lengths = tables[1]
    chosen_row = tables[2]
    device_ids = jnp.arange(MESH_DEVICES, dtype=jnp.int32)[:, None]
    grid_row = device_ids // GRID_COLS
    grid_col = device_ids % GRID_COLS
    owners = jax.random.randint(jax.random.fold_in(key, 23), (MESH_DEVICES, TILES_DEV), 0, GRID_COLS)
    raw_bits = jax.random.randint(jax.random.fold_in(key, 24), (MESH_DEVICES, TILES_DEV), 0, 1 << 20)
    available = lengths[(grid_row * GRID_COLS + owners) * GRID_COLS + grid_col]
    slots = owners * CAPO + raw_bits % available
    positions = jnp.arange(TILES_DEV, dtype=jnp.int32)[None, :]
    marked = device_ids == chosen_row * GRID_COLS
    slots = jnp.where(marked & (positions == 0), ROW_SLOTS - 1, slots)
    slots = jnp.where(marked & (positions == 1), 0, slots)
    return slots.reshape(-1).astype(jnp.int32)


def draw_tile_count(key, part):
    halvings = jax.random.randint(jax.random.fold_in(key, 31), (MESH_DEVICES,), 0, 4)
    base_count = jnp.right_shift(jnp.int32(TILES_DEV), halvings)
    spread = jnp.maximum(1, jnp.right_shift(jnp.int32(TILES_DEV), halvings + 2))
    jitter = jax.random.randint(jax.random.fold_in(key, 32), (MESH_DEVICES,), 0, 1 << 20) % spread
    counts = base_count - jitter
    chosen = jax.random.randint(jax.random.fold_in(key, 33), (), 0, MESH_DEVICES)
    counts = jnp.where(jnp.arange(MESH_DEVICES, dtype=jnp.int32) == chosen, TILES_DEV, counts)
    return counts.astype(jnp.int32)


def block_levels(rng, shape, pieces, least, top_value):
    loudness = 1.0
    for dim, shards_of in pieces:
        steps = jax.random.uniform(jax.random.fold_in(jax.random.fold_in(rng, 6), dim), (shards_of,), jnp.float32, least / len(pieces), top_value / len(pieces))
        loudness = loudness * jnp.repeat(jnp.exp(steps), shape[dim] // shards_of).reshape((-1,) + (1,) * (len(shape) - 1 - dim))
    return loudness


def scatter_about(own_key, dims, scale, reach, split=(), kind=jnp.bfloat16):
    drawn = jax.random.normal(own_key, dims, jnp.float32) * scale
    if len(split) > 0:
        drawn = block_levels(own_key, dims, split, -0.22, 0.18) * drawn
    return jnp.clip(drawn, min=-reach, max=reach).astype(kind)


def setup_inputs(seed: int = 0) -> dict:
    key_of = jax.random.split(jax.random.key(seed), 11)
    return {
        "features": scatter_about(key_of[0], (NODES, F), 1.0, 6.0, ((0, 32),)),
        "weight": scatter_about(key_of[1], (F, F), F ** -0.5, 0.375),
        "layer_bias": scatter_about(key_of[2], (F,), 0.5, 3.0, (), jnp.float32),
        "adj_tiles": jnp.clip(0.079589844 * jax.random.uniform(key_of[3], (MESH_DEVICES * TILES_DEV, TILE, TILE), jnp.float32) ** block_levels(key_of[3], (MESH_DEVICES * TILES_DEV, TILE, TILE), ((0, 32),), -0.2, 0.2), 0.0, 0.079589844).astype(jnp.bfloat16),
        "tile_source": draw_tile_source(jax.random.fold_in(key_of[10], 71), 0),
        "tile_target": draw_tile_target(jax.random.fold_in(key_of[10], 71), 0),
        "tile_count": draw_tile_count(jax.random.fold_in(key_of[10], 71), 0),
        "fetch_list": draw_fetch_list(jax.random.fold_in(key_of[10], 71), 0),
        "deliver_list": draw_deliver_list(jax.random.fold_in(key_of[10], 71), 0),
        "cotangent": scatter_about(key_of[9], (NODES, F), 1.0, 6.0, ((0, 32),)),
    }


def silu_grad(values):
    logistic = jax.nn.sigmoid(values)
    return logistic * (1.0 + values * (1.0 - logistic))

def slot_blocks(fetch_list, deliver_list):
    device_ids = jnp.arange(MESH_DEVICES, dtype=jnp.int32)
    grid_row = device_ids // GRID_COLS
    grid_col = device_ids % GRID_COLS
    src_owner = jnp.arange(GRID_ROWS, dtype=jnp.int32)[None, :] * GRID_COLS + grid_col[:, None]
    src_entry = fetch_list.reshape(MESH_DEVICES, GRID_ROWS, CAPF)
    src_block = jnp.where(src_entry >= 0, src_owner[:, :, None] * BLK_DEV + src_entry, -1)
    row_owner = grid_row[:, None] * GRID_COLS + jnp.arange(GRID_COLS, dtype=jnp.int32)[None, :]
    row_entry = deliver_list[row_owner * GRID_COLS + grid_col[:, None]]
    row_block = jnp.where(row_entry >= 0, row_owner[:, :, None] * BLK_DEV + row_entry, -1)
    return (src_block.reshape(MESH_DEVICES, SRC_SLOTS).astype(jnp.int32), row_block.reshape(MESH_DEVICES, ROW_SLOTS).astype(jnp.int32))

def reference(features, weight, layer_bias, adj_tiles, tile_source, tile_target, tile_count, fetch_list, deliver_list, cotangent):
    block_total = NODES // TILE
    projected = jnp.dot(features, weight, preferred_element_type=jnp.float32).astype(jnp.bfloat16)
    proj_blocks = projected.reshape(block_total, TILE, F)
    src_block, row_block = slot_blocks(fetch_list, deliver_list)
    tile_sets = adj_tiles.reshape(MESH_DEVICES, TILES_DEV, TILE, TILE)
    sources = tile_source.reshape(MESH_DEVICES, TILES_DEV)
    targets = tile_target.reshape(MESH_DEVICES, TILES_DEV)
    positions = jnp.arange(TILES_DEV, dtype=jnp.int32)
    device_items = (tile_sets, sources, targets, tile_count, src_block, row_block)

    def forward_step(running, device_item):
        tile_set, source, target, live_count, src_ids, row_ids = device_item
        picked = proj_blocks[jnp.maximum(src_ids[source], 0)].astype(jnp.float32)
        products = jnp.einsum('kij,kjf->kif', tile_set.astype(jnp.float32), picked)
        products = jnp.where((positions < live_count)[:, None, None], products, jnp.zeros_like(products))
        slot_sums = jax.ops.segment_sum(products, target, num_segments=ROW_SLOTS)
        slot_sums = lax.optimization_barrier(slot_sums.astype(jnp.bfloat16)).astype(jnp.float32)
        where_to = jnp.where(row_ids >= 0, row_ids, block_total).astype(jnp.int32)
        return (running.at[where_to].add(slot_sums, mode='drop'), None)
    aggregated, unused = lax.scan(forward_step, jnp.zeros((block_total, TILE, F), jnp.float32), device_items)
    pre_act = aggregated.reshape(NODES, F) + layer_bias
    layer_out = jax.nn.silu(pre_act).astype(jnp.bfloat16)
    slopes = cotangent.astype(jnp.float32) * silu_grad(pre_act)
    slope_blocks = slopes.astype(jnp.bfloat16).reshape(block_total, TILE, F)

    def backward_step(running, device_item):
        tile_set, source, target, live_count, src_ids, row_ids = device_item
        picked = slope_blocks[jnp.maximum(row_ids[target], 0)].astype(jnp.float32)
        products = jnp.einsum('kji,kjf->kif', tile_set.astype(jnp.float32), picked)
        products = jnp.where((positions < live_count)[:, None, None], products, jnp.zeros_like(products))
        slot_sums = jax.ops.segment_sum(products, source, num_segments=SRC_SLOTS)
        slot_sums = lax.optimization_barrier(slot_sums.astype(jnp.bfloat16)).astype(jnp.float32)
        where_to = jnp.where(src_ids >= 0, src_ids, block_total).astype(jnp.int32)
        return (running.at[where_to].add(slot_sums, mode='drop'), None)
    backward, unused = lax.scan(backward_step, jnp.zeros((block_total, TILE, F), jnp.float32), device_items)
    grad_proj = backward.reshape(NODES, F).astype(jnp.bfloat16)
    grad_features = jnp.dot(grad_proj, weight.T, preferred_element_type=jnp.float32).astype(jnp.bfloat16)
    grad_scale = NODES ** (-0.5)
    grad_weight = jnp.dot(features.T, grad_proj, preferred_element_type=jnp.float32) * grad_scale
    grad_bias = lax.optimization_barrier(jnp.sum(slopes, axis=0)) * grad_scale
    return (layer_out, grad_features, grad_weight, grad_bias)
```

```python
import functools
import math

import jax
import jax.numpy as jnp
from jax import lax
from jax.experimental import pallas as pl
from jax.experimental.pallas import tpu as pltpu
from jax.sharding import PartitionSpec as P

F32 = jnp.float32
BF16 = jnp.bfloat16
HALVES = 2


def loop(lower, upper, step):
    def run(i, carry):
        step(i)
        return carry

    lax.fori_loop(lower, upper, run, 0)


def layer_kernel(
    R,
    C,
    fuse_sum,
    scale,
    take_src,
    take_row,
    prev_row,
    last_row,
    prev_src,
    last_src,
    deliver,
    features,
    weight,
    bias,
    tiles,
    lists,
    cotangent,
    layer_out,
    grad_features,
    grad_weight,
    grad_bias,
    *scratch,
):
    H = HALVES
    scratch = list(scratch)

    def take(count):
        taken = scratch[:count]
        del scratch[:count]
        return taken

    (list_all, proj, fetch_out, prod, turned, agg, proj_grad) = take(7)
    src = take(H)
    rows_out = take(H)
    rows_in = take(H)
    slope = take(H)
    slope_out = take(H)
    row_vals = take(H)
    back_out = take(H)
    back_in = take(H)
    (term, bias_acc, bias_row, bias_in1, bias_mid, bias_in2) = take(6)
    (part_in, part_sum, piece_in, piece_sum, piece_all, part_all) = take(6)
    (list_s, list_r, fetch_s, fetch_r, rows_s, rows_r) = take(6)
    (slope_s, slope_r, back_s, back_r, b1_s, b1_r, b2_s, b2_r) = take(8)
    (p1_s, p1_r, p2_s, p2_r, p3_s, p3_r, p4_s, p4_r) = take(8)

    r = lax.axis_index("row")
    c = lax.axis_index("col")
    T = tiles.shape[0]
    side = tiles.shape[1]
    B = proj.shape[1]
    FC = proj.shape[3]
    CF = fetch_out.shape[2]
    CO = rows_out[0].shape[1]

    def row_copy(source, target, send, recv, q):
        return pltpu.make_async_remote_copy(
            source, target, send, recv, device_id={"row": q}, device_id_type=pl.DeviceIdType.MESH
        )

    def col_copy(source, target, send, recv, p):
        return pltpu.make_async_remote_copy(
            source, target, send, recv, device_id={"col": p}, device_id_type=pl.DeviceIdType.MESH
        )

    def row_peers(step):
        loop(1, R, lambda i: step(lax.rem(r + i, R)))

    def col_peers(step):
        loop(1, C, lambda i: step(lax.rem(c + i, C)))

    barrier = pltpu.get_barrier_semaphore()
    row_peers(
        lambda q: pl.semaphore_signal(
            barrier, inc=1, device_id={"row": q}, device_id_type=pl.DeviceIdType.MESH
        )
    )
    col_peers(
        lambda p: pl.semaphore_signal(
            barrier, inc=1, device_id={"col": p}, device_id_type=pl.DeviceIdType.MESH
        )
    )
    pl.semaphore_wait(barrier, R + C - 2)

    row_peers(
        lambda q: row_copy(
            lists.at[q], list_all.at[r], list_s.at[q], list_r.at[r], q
        ).start()
    )
    list_all[r] = lists[r]

    def project(b):
        rows = pl.ds(pl.multiple_of(b * side, side), side)
        whole = jnp.dot(features[rows, :], weight[...], preferred_element_type=F32).astype(BF16)
        for h in range(H):
            proj[h, b] = whole[:, h * FC : (h + 1) * FC]

    loop(0, B, project)
    row_peers(
        lambda q: row_copy(
            lists.at[q], list_all.at[q], list_s.at[q], list_r.at[q], q
        ).wait_recv()
    )

    def picked(h, q, j):
        wanted = list_all[q, j : j + 1, :FC]
        total = jnp.zeros((side, FC), F32)
        for b in range(B):
            total = total + (wanted == b).astype(F32) * proj[h, b].astype(F32)
        return total.astype(BF16)

    def fetch_copy(h, q, frm):
        return row_copy(
            fetch_out.at[h, q], src[h].at[frm], fetch_s.at[h, q], fetch_r.at[h, frm], q
        )

    for h in range(H):

        def send_fetch(q, h=h):
            for j in range(CF):
                fetch_out[h, q, j] = picked(h, q, j)
            fetch_copy(h, q, r).start()

        row_peers(send_fetch)
        for j in range(CF):
            src[h][r, j] = picked(h, r, j)

    prod[T] = jnp.zeros((side, FC), F32)

    def clear(b):
        for h in range(H):
            agg[h, b] = jnp.zeros((side, FC), F32)

    loop(0, B, clear)

    group = math.gcd(T, 8)

    def tile_sums(left, right, index, cap, prev):
        def multiply(g):
            for u in range(group):
                k = g * group + u
                slot = index[k]
                prod[k] = jnp.dot(
                    left[k], right[slot // cap, lax.rem(slot, cap)], preferred_element_type=F32
                )

        loop(0, T // group, multiply)

        def chain(k):
            prod[k] = prod[k] + prod[prev[k]]

        loop(0, T, chain)

    def rows_copy(h, p, frm):
        return col_copy(
            rows_out[h].at[p], rows_in[h].at[frm], rows_s.at[h, p], rows_r.at[h, frm], p
        )

    for h in range(H):
        row_peers(lambda q, h=h: fetch_copy(h, q, q).wait_recv())
        tile_sums(tiles, src[h], take_src, CF, prev_row)

        def send_rows(p, h=h):
            for j in range(CO):
                rows_out[h][p, j] = prod[last_row[p * CO + j]].astype(BF16)
            rows_copy(h, p, c).start()

        col_peers(send_rows)
        for j in range(CO):
            rows_in[h][c, j] = prod[last_row[c * CO + j]].astype(BF16)

    def turn(g):
        for u in range(group):
            turned[g * group + u] = tiles[g * group + u].T

    loop(0, T // group, turn)

    strip = 16

    def add_rows(h, p):
        masks = [
            [(deliver[p * CO + j] == b).astype(F32) for j in range(CO)] for b in range(B)
        ]

        def add(i):
            rows = pl.ds(pl.multiple_of(i * strip, strip), strip)
            got = [rows_in[h][p, j, rows, :].astype(F32) for j in range(CO)]
            for b in range(B):
                total = agg[h, b, rows, :]
                for j in range(CO):
                    total = total + masks[b][j] * got[j]
                agg[h, b, rows, :] = total

        loop(0, side // strip, add)

    def slope_copy(h, p, frm):
        return col_copy(
            slope_out[h].at[p], row_vals[h].at[frm], slope_s.at[h, p], slope_r.at[h, frm], p
        )

    bias_acc[...] = jnp.zeros_like(bias_acc)
    for h in range(H):
        cols = slice(h * FC, (h + 1) * FC)
        add_rows(h, c)

        def arrive(p, h=h):
            rows_copy(h, p, p).wait_recv()
            add_rows(h, p)

        col_peers(arrive)

        def activate(b, h=h, cols=cols):
            rows = pl.ds(pl.multiple_of(b * side, side), side)
            value = agg[h, b] + bias[0:1, cols]
            logistic = 1.0 / (1.0 + jnp.exp(-value))
            layer_out[rows, cols] = (value * logistic).astype(BF16)
            grad = cotangent[rows, cols].astype(F32) * (
                logistic * (1.0 + value * (1.0 - logistic))
            )
            slope[h][b] = grad.astype(BF16)
            bias_acc[:, cols] = bias_acc[:, cols] + jnp.sum(
                grad.reshape(side // 8, 8, FC), axis=0
            )

        loop(0, B, activate)

        def send_slope(p, h=h):
            for j in range(CO):
                slope_out[h][p, j] = slope[h][jnp.maximum(deliver[p * CO + j], 0)]
            slope_copy(h, p, c).start()

        col_peers(send_slope)
        for j in range(CO):
            row_vals[h][c, j] = slope[h][jnp.maximum(deliver[c * CO + j], 0)]

    bias_row[...] = bias_acc[...]

    def bias1(q, frm):
        return row_copy(bias_row, bias_in1.at[frm], b1_s.at[q], b1_r.at[frm], q)

    def bias2(p, frm):
        return col_copy(bias_mid, bias_in2.at[frm], b2_s.at[p], b2_r.at[frm], p)

    row_peers(lambda q: bias1(q, r).start())
    bias_in1[r] = bias_acc[...]

    def back_copy(h, q, frm):
        return row_copy(
            back_out[h].at[q], back_in[h].at[frm], back_s.at[h, q], back_r.at[h, frm], q
        )

    for h in range(H):
        col_peers(lambda p, h=h: slope_copy(h, p, p).wait_recv())
        tile_sums(turned, row_vals[h], take_row, CO, prev_src)

        def send_back(q, h=h):
            for j in range(CF):
                back_out[h][q, j] = prod[last_src[q * CF + j]].astype(BF16)
            back_copy(h, q, r).start()

        row_peers(send_back)
        for j in range(CF):
            back_in[h][r, j] = prod[last_src[r * CF + j]].astype(BF16)
        if h == 0:
            row_peers(lambda q: bias1(q, q).wait_recv())
            bias_mid[...] = jnp.sum(bias_in1[...], axis=0)
            col_peers(lambda p: bias2(p, c).start())
            bias_in2[c] = bias_mid[...]

    for h in range(H):
        cols = slice(h * FC, (h + 1) * FC)
        row_peers(lambda q, h=h: back_copy(h, q, q).wait_recv())

        def gather_back(b, h=h, cols=cols):
            total = jnp.zeros((side, FC), F32)
            for q in range(R):
                for j in range(CF):
                    mask = (list_all[q, j : j + 1, :FC] == b).astype(F32)
                    total = total + mask * back_in[h][q, j].astype(F32)
            rows = pl.ds(pl.multiple_of(b * side, side), side)
            proj_grad[rows, cols] = total.astype(BF16)

        loop(0, B, gather_back)

    term[...] = lax.dot_general(
        features[...], proj_grad[...], (((0,), (0,)), ((), ())), preferred_element_type=F32
    )

    F = weight.shape[0]
    half = F // R
    piece = half // C

    def part1(q, frm):
        place = pl.ds(pl.multiple_of(q * half, 8), half)
        return row_copy(term.at[place, :], part_in.at[frm], p1_s.at[q], p1_r.at[frm], q)

    def part2(p, frm):
        place = pl.ds(pl.multiple_of(p * piece, 8), piece)
        return col_copy(part_sum.at[place, :], piece_in.at[frm], p2_s.at[p], p2_r.at[frm], p)

    def part3(p, frm):
        return col_copy(piece_sum, piece_all.at[frm], p3_s.at[p], p3_r.at[frm], p)

    def part4(q, frm):
        return row_copy(piece_all, part_all.at[frm], p4_s.at[q], p4_r.at[frm], q)

    if fuse_sum:
        row_peers(lambda q: part1(q, r).start())
        part_in[r] = term[pl.ds(pl.multiple_of(r * half, 8), half), :]

    def features_back(b):
        rows = pl.ds(pl.multiple_of(b * side, side), side)
        grad_features[rows, :] = lax.dot_general(
            proj_grad[rows, :], weight[...], (((1,), (1,)), ((), ())), preferred_element_type=F32
        ).astype(BF16)

    loop(0, B, features_back)
    col_peers(lambda p: bias2(p, p).wait_recv())
    grad_bias[...] = jnp.broadcast_to(
        jnp.sum(jnp.sum(bias_in2[...], axis=0), axis=0, keepdims=True) * scale, grad_bias.shape
    )

    if fuse_sum:
        row_peers(lambda q: part1(q, q).wait_recv())
        part_sum[...] = jnp.sum(part_in[...], axis=0)
        col_peers(lambda p: part2(p, c).start())
        piece_in[c] = part_sum[pl.ds(pl.multiple_of(c * piece, 8), piece), :]
        col_peers(lambda p: part2(p, p).wait_recv())
        piece_sum[...] = jnp.sum(piece_in[...], axis=0) * scale
        col_peers(lambda p: part3(p, c).start())
        piece_all[c] = piece_sum[...]
        col_peers(lambda p: part3(p, p).wait_recv())
        row_peers(lambda q: part4(q, r).start())
        part_all[r] = piece_all[...]
        row_peers(lambda q: part4(q, q).wait_recv())
        grad_weight[...] = part_all[...].reshape(F, F)
        row_peers(lambda q: part1(q, r).wait_send())
        col_peers(lambda p: part2(p, c).wait_send())
        col_peers(lambda p: part3(p, c).wait_send())
        row_peers(lambda q: part4(q, r).wait_send())
    else:
        grad_weight[...] = term[...]

    row_peers(
        lambda q: row_copy(
            lists.at[q], list_all.at[r], list_s.at[q], list_r.at[r], q
        ).wait_send()
    )
    row_peers(lambda q: bias1(q, r).wait_send())
    col_peers(lambda p: bias2(p, c).wait_send())
    for h in range(H):
        row_peers(lambda q, h=h: fetch_copy(h, q, r).wait_send())
        col_peers(lambda p, h=h: rows_copy(h, p, c).wait_send())
        col_peers(lambda p, h=h: slope_copy(h, p, c).wait_send())
        row_peers(lambda q, h=h: back_copy(h, q, r).wait_send())


def chains(slots, live, slot_total):
    tile_total = slots.shape[0]
    ids = jnp.arange(tile_total, dtype=jnp.int32)
    same = (slots[None, :] == slots[:, None]) & (ids[None, :] < ids[:, None])
    prev = jnp.max(jnp.where(same, ids[None, :], -1), axis=1)
    slot_ids = jnp.arange(slot_total, dtype=jnp.int32)
    here = (slots[None, :] == slot_ids[:, None]) & (ids[None, :] < live)
    last = jnp.max(jnp.where(here, ids[None, :], -1), axis=1)
    return (
        jnp.where(prev < 0, tile_total, prev).astype(jnp.int32),
        jnp.where(last < 0, tile_total, last).astype(jnp.int32),
    )


def body(
    features,
    weight,
    layer_bias,
    adj_tiles,
    tile_source,
    tile_target,
    tile_count,
    fetch_list,
    deliver_list,
    cotangent,
):
    R = lax.axis_size("row")
    C = lax.axis_size("col")
    H = HALVES
    N, F = features.shape
    T, side, _ = adj_tiles.shape
    B = N // side
    CF = fetch_list.shape[1]
    CO = deliver_list.shape[1]
    FC = F // H
    half = F // R
    piece = half // C
    fuse_sum = F % R == 0 and half % C == 0 and piece % 8 == 0
    scale = 1.0 / math.sqrt(N * R * C)
    live = tile_count[0]
    prev_row, last_row = chains(tile_target, live, C * CO)
    prev_src, last_src = chains(tile_source, live, R * CF)
    list_rows = -(-CF // 8) * 8
    lists = jnp.broadcast_to(
        jnp.pad(fetch_list, ((0, 0), (0, list_rows - CF)), constant_values=-1)[:, :, None],
        (R, list_rows, F),
    )
    V = pltpu.VMEM
    dma = pltpu.SemaphoreType.DMA
    small = piece if fuse_sum else 8
    scratch = [
        V((R, list_rows, F), jnp.int32),
        V((H, B, side, FC), BF16),
        V((H, R, CF, side, FC), BF16),
        V((T + 1, side, FC), F32),
        V((T, side, side), BF16),
        V((H, B, side, FC), F32),
        V((N, F), BF16),
        *[V((R, CF, side, FC), BF16)] * H,
        *[V((C, CO, side, FC), BF16)] * H,
        *[V((C, CO, side, FC), BF16)] * H,
        *[V((B, side, FC), BF16)] * H,
        *[V((C, CO, side, FC), BF16)] * H,
        *[V((C, CO, side, FC), BF16)] * H,
        *[V((R, CF, side, FC), BF16)] * H,
        *[V((R, CF, side, FC), BF16)] * H,
        V((F, F), F32),
        V((8, F), F32),
        V((8, F), F32),
        V((R, 8, F), F32),
        V((8, F), F32),
        V((C, 8, F), F32),
        V((R, half, F), F32),
        V((half, F), F32),
        V((C, small, F), F32),
        V((small, F), F32),
        V((C, small, F), F32),
        V((R, C, small, F), F32),
        *[dma((R,))] * 2,
        *[dma((H, R))] * 2,
        *[dma((H, C))] * 2,
        *[dma((H, C))] * 2,
        *[dma((H, R))] * 2,
        *[dma((R,))] * 2,
        *[dma((C,))] * 2,
        *[dma((R,))] * 2,
        *[dma((C,))] * 2,
        *[dma((C,))] * 2,
        *[dma((R,))] * 2,
    ]
    vmem = pl.BlockSpec(memory_space=pltpu.VMEM)
    smem = pl.BlockSpec(memory_space=pltpu.SMEM)
    layer_out, grad_features, grad_weight, grad_bias = pl.pallas_call(
        functools.partial(layer_kernel, R, C, fuse_sum, scale),
        out_shape=(
            jax.ShapeDtypeStruct((N, F), BF16),
            jax.ShapeDtypeStruct((N, F), BF16),
            jax.ShapeDtypeStruct((F, F), F32),
            jax.ShapeDtypeStruct((8, F), F32),
        ),
        in_specs=[smem] * 7 + [vmem] * 6,
        out_specs=(vmem,) * 4,
        scratch_shapes=scratch,
        compiler_params=pltpu.CompilerParams(
            collective_id=0, has_side_effects=True, vmem_limit_bytes=56 * 1024 * 1024
        ),
    )(
        tile_source,
        tile_target,
        prev_row,
        last_row,
        prev_src,
        last_src,
        deliver_list.reshape(-1),
        features,
        weight,
        layer_bias.reshape(1, F),
        adj_tiles,
        lists,
        cotangent,
    )
    grad_bias = grad_bias[0]
    if not fuse_sum:
        grad_weight = lax.psum(grad_weight, ("row", "col")) * scale
    return (layer_out, grad_features, grad_weight, grad_bias)


def solution(mesh):
    return jax.shard_map(
        body,
        mesh=mesh,
        in_specs=(
            P(("row", "col"), None),
            P(),
            P(),
            P(("row", "col"), None, None),
            P(("row", "col")),
            P(("row", "col")),
            P(("row", "col")),
            P(("row", "col"), None),
            P(("row", "col"), None),
            P(("row", "col"), None),
        ),
        out_specs=(P(("row", "col"), None), P(("row", "col"), None), P(), P()),
        check_vma=False,
    )
```

```python
import functools
import math

import jax
import jax.numpy as jnp
from jax import lax
from jax.experimental import pallas as pl
from jax.experimental.pallas import tpu as pltpu
from jax.sharding import PartitionSpec as P

F32 = jnp.float32
BF16 = jnp.bfloat16
HALVES = 2


def loop(lower, upper, step):
    def run(i, carry):
        step(i)
        return carry

    lax.fori_loop(lower, upper, run, 0)


def layer_kernel(
    R,
    C,
    fuse_sum,
    scale,
    take_src,
    take_row,
    prev_row,
    last_row,
    prev_src,
    last_src,
    fetch,
    deliver,
    features,
    weight,
    bias,
    tiles_hbm,
    cotangent_hbm,
    layer_out_hbm,
    grad_features,
    grad_weight,
    grad_bias,
    *scratch,
):
    H = HALVES
    scratch = list(scratch)

    def take(count):
        taken = scratch[:count]
        del scratch[:count]
        return taken

    (tiles, cotangent, layer_out, lists) = take(4)
    (list_all, proj, fetch_out, prod, turned, agg, proj_grad) = take(7)
    src = take(H)
    rows_out = take(H)
    rows_in = take(H)
    slope = take(H)
    slope_out = take(H)
    row_vals = take(H)
    back_out = take(H)
    back_in = take(H)
    (term, bias_acc, bias_row, bias_in1, bias_mid, bias_in2) = take(6)
    (part_in, part_sum, piece_in, piece_sum, piece_all, part_all) = take(6)
    (list_s, list_r, fetch_s, fetch_r, rows_s, rows_r) = take(6)
    (slope_s, slope_r, back_s, back_r, b1_s, b1_r, b2_s, b2_r) = take(8)
    (p1_s, p1_r, p2_s, p2_r, p3_s, p3_r, p4_s, p4_r, local) = take(9)

    r = lax.axis_index("row")
    c = lax.axis_index("col")
    T = tiles.shape[0]
    side = tiles.shape[1]
    B = proj.shape[1]
    FC = proj.shape[3]
    CF = fetch_out.shape[2]
    CO = rows_out[0].shape[1]

    def row_copy(source, target, send, recv, q):
        return pltpu.make_async_remote_copy(
            source, target, send, recv, device_id={"row": q}, device_id_type=pl.DeviceIdType.MESH
        )

    def col_copy(source, target, send, recv, p):
        return pltpu.make_async_remote_copy(
            source, target, send, recv, device_id={"col": p}, device_id_type=pl.DeviceIdType.MESH
        )

    def row_peers(step):
        loop(1, R, lambda i: step(lax.rem(r + i, R)))

    def col_peers(step):
        loop(1, C, lambda i: step(lax.rem(c + i, C)))

    barrier = pltpu.get_barrier_semaphore()
    row_peers(
        lambda q: pl.semaphore_signal(
            barrier, inc=1, device_id={"row": q}, device_id_type=pl.DeviceIdType.MESH
        )
    )
    col_peers(
        lambda p: pl.semaphore_signal(
            barrier, inc=1, device_id={"col": p}, device_id_type=pl.DeviceIdType.MESH
        )
    )
    tiles_copy = pltpu.make_async_copy(tiles_hbm, tiles, local.at[0])
    cotangent_copy = pltpu.make_async_copy(cotangent_hbm, cotangent, local.at[1])
    out_copy = pltpu.make_async_copy(layer_out, layer_out_hbm, local.at[2])
    tiles_copy.start()
    cotangent_copy.start()
    lists[...] = jnp.full(lists.shape, -1, jnp.int32)
    for q in range(R):
        for j in range(CF):
            row = jnp.zeros((1, lists.shape[2]), jnp.int32) + fetch[q, j]
            lists[q, j : j + 1, :] = row
    pl.semaphore_wait(barrier, R + C - 2)

    row_peers(
        lambda q: row_copy(
            lists.at[q], list_all.at[r], list_s.at[q], list_r.at[r], q
        ).start()
    )
    list_all[r] = lists[r]

    def project(b):
        rows = pl.ds(pl.multiple_of(b * side, side), side)
        whole = jnp.dot(features[rows, :], weight[...], preferred_element_type=F32).astype(BF16)
        for h in range(H):
            proj[h, b] = whole[:, h * FC : (h + 1) * FC]

    loop(0, B, project)
    row_peers(
        lambda q: row_copy(
            lists.at[q], list_all.at[q], list_s.at[q], list_r.at[q], q
        ).wait_recv()
    )

    def picked(h, q, j):
        wanted = list_all[q, j : j + 1, :FC]
        total = jnp.zeros((side, FC), F32)
        for b in range(B):
            total = total + (wanted == b).astype(F32) * proj[h, b].astype(F32)
        return total.astype(BF16)

    def fetch_copy(h, q, frm):
        return row_copy(
            fetch_out.at[h, q], src[h].at[frm], fetch_s.at[h, q], fetch_r.at[h, frm], q
        )

    for h in range(H):

        def send_fetch(q, h=h):
            for j in range(CF):
                fetch_out[h, q, j] = picked(h, q, j)
            fetch_copy(h, q, r).start()

        row_peers(send_fetch)
        for j in range(CF):
            src[h][r, j] = picked(h, r, j)

    prod[T] = jnp.zeros((side, FC), F32)

    def clear(b):
        for h in range(H):
            agg[h, b] = jnp.zeros((side, FC), F32)

    loop(0, B, clear)

    group = math.gcd(T, 8)

    def tile_sums(left, right, index, cap, prev):
        def multiply(g):
            for u in range(group):
                k = g * group + u
                slot = index[k]
                prod[k] = jnp.dot(
                    left[k], right[slot // cap, lax.rem(slot, cap)], preferred_element_type=F32
                )

        loop(0, T // group, multiply)

        def chain(k):
            prod[k] = prod[k] + prod[prev[k]]

        loop(0, T, chain)

    def rows_copy(h, p, frm):
        return col_copy(
            rows_out[h].at[p], rows_in[h].at[frm], rows_s.at[h, p], rows_r.at[h, frm], p
        )

    tiles_copy.wait()
    for h in range(H):
        row_peers(lambda q, h=h: fetch_copy(h, q, q).wait_recv())
        tile_sums(tiles, src[h], take_src, CF, prev_row)

        def send_rows(p, h=h):
            for j in range(CO):
                rows_out[h][p, j] = prod[last_row[p * CO + j]].astype(BF16)
            rows_copy(h, p, c).start()

        col_peers(send_rows)
        for j in range(CO):
            rows_in[h][c, j] = prod[last_row[c * CO + j]].astype(BF16)

    def turn(g):
        for u in range(group):
            turned[g * group + u] = tiles[g * group + u].T

    loop(0, T // group, turn)

    strip = 16

    def add_rows(h, p):
        masks = [
            [(deliver[p, j] == b).astype(F32) for j in range(CO)] for b in range(B)
        ]

        def add(i):
            rows = pl.ds(pl.multiple_of(i * strip, strip), strip)
            got = [rows_in[h][p, j, rows, :].astype(F32) for j in range(CO)]
            for b in range(B):
                total = agg[h, b, rows, :]
                for j in range(CO):
                    total = total + masks[b][j] * got[j]
                agg[h, b, rows, :] = total

        loop(0, side // strip, add)

    def slope_copy(h, p, frm):
        return col_copy(
            slope_out[h].at[p], row_vals[h].at[frm], slope_s.at[h, p], slope_r.at[h, frm], p
        )

    bias_acc[...] = jnp.zeros_like(bias_acc)
    cotangent_copy.wait()
    for h in range(H):
        cols = slice(h * FC, (h + 1) * FC)
        add_rows(h, c)

        def arrive(p, h=h):
            rows_copy(h, p, p).wait_recv()
            add_rows(h, p)

        col_peers(arrive)

        def activate(b, h=h, cols=cols):
            rows = pl.ds(pl.multiple_of(b * side, side), side)
            value = agg[h, b] + bias[0:1, cols]
            logistic = 1.0 / (1.0 + jnp.exp(-value))
            layer_out[rows, cols] = (value * logistic).astype(BF16)
            grad = cotangent[rows, cols].astype(F32) * (
                logistic * (1.0 + value * (1.0 - logistic))
            )
            slope[h][b] = grad.astype(BF16)
            bias_acc[:, cols] = bias_acc[:, cols] + jnp.sum(
                grad.reshape(side // 8, 8, FC), axis=0
            )

        loop(0, B, activate)

        def send_slope(p, h=h):
            for j in range(CO):
                slope_out[h][p, j] = slope[h][jnp.maximum(deliver[p, j], 0)]
            slope_copy(h, p, c).start()

        col_peers(send_slope)
        for j in range(CO):
            row_vals[h][c, j] = slope[h][jnp.maximum(deliver[c, j], 0)]

    out_copy.start()

    bias_row[...] = bias_acc[...]

    def bias1(q, frm):
        return row_copy(bias_row, bias_in1.at[frm], b1_s.at[q], b1_r.at[frm], q)

    def bias2(p, frm):
        return col_copy(bias_mid, bias_in2.at[frm], b2_s.at[p], b2_r.at[frm], p)

    row_peers(lambda q: bias1(q, r).start())
    bias_in1[r] = bias_acc[...]

    def back_copy(h, q, frm):
        return row_copy(
            back_out[h].at[q], back_in[h].at[frm], back_s.at[h, q], back_r.at[h, frm], q
        )

    F = weight.shape[0]
    half = F // R
    piece = half // C

    def part1(h, q, frm):
        place = pl.ds(pl.multiple_of(q * half, 8), half)
        return row_copy(
            term.at[h, place, :], part_in.at[h, frm], p1_s.at[h, q], p1_r.at[h, frm], q
        )

    def part2(h, p, frm):
        place = pl.ds(pl.multiple_of(p * piece, 8), piece)
        return col_copy(
            part_sum.at[h, place, :], piece_in.at[h, frm], p2_s.at[h, p], p2_r.at[h, frm], p
        )

    def part3(h, p, frm):
        return col_copy(piece_sum.at[h], piece_all.at[h, frm], p3_s.at[h, p], p3_r.at[h, frm], p)

    def part4(h, q, frm):
        return row_copy(piece_all.at[h], part_all.at[h, frm], p4_s.at[h, q], p4_r.at[h, frm], q)

    def sum1(h):
        if fuse_sum:
            row_peers(lambda q: part1(h, q, r).start())
            part_in[h, r] = term[h, pl.ds(pl.multiple_of(r * half, 8), half), :]

    def sum2(h):
        if fuse_sum:
            row_peers(lambda q: part1(h, q, q).wait_recv())
            part_sum[h] = jnp.sum(part_in[h], axis=0)
            col_peers(lambda p: part2(h, p, c).start())
            piece_in[h, c] = part_sum[h, pl.ds(pl.multiple_of(c * piece, 8), piece), :]

    def sum3(h):
        if fuse_sum:
            col_peers(lambda p: part2(h, p, p).wait_recv())
            piece_sum[h] = jnp.sum(piece_in[h], axis=0) * scale
            col_peers(lambda p: part3(h, p, c).start())
            piece_all[h, c] = piece_sum[h]

    def sum4(h):
        if fuse_sum:
            col_peers(lambda p: part3(h, p, p).wait_recv())
            row_peers(lambda q: part4(h, q, r).start())
            part_all[h, r] = piece_all[h]

    def sum5(h):
        cols = slice(h * FC, (h + 1) * FC)
        if fuse_sum:
            row_peers(lambda q: part4(h, q, q).wait_recv())
            grad_weight[:, cols] = part_all[h].reshape(F, FC)
        else:
            grad_weight[:, cols] = term[h]

    def source_part(h):
        col_peers(lambda p: slope_copy(h, p, p).wait_recv())
        if h > 0:
            sum2(h - 1)
        tile_sums(turned, row_vals[h], take_row, CO, prev_src)

        def send_back(q):
            for j in range(CF):
                back_out[h][q, j] = prod[last_src[q * CF + j]].astype(BF16)
            back_copy(h, q, r).start()

        row_peers(send_back)
        for j in range(CF):
            back_in[h][r, j] = prod[last_src[r * CF + j]].astype(BF16)

    def weight_part(h):
        cols = slice(h * FC, (h + 1) * FC)
        row_peers(lambda q: back_copy(h, q, q).wait_recv())

        def gather_back(b):
            total = jnp.zeros((side, FC), F32)
            for q in range(R):
                for j in range(CF):
                    mask = (list_all[q, j : j + 1, :FC] == b).astype(F32)
                    total = total + mask * back_in[h][q, j].astype(F32)
            rows = pl.ds(pl.multiple_of(b * side, side), side)
            proj_grad[rows, cols] = total.astype(BF16)

        loop(0, B, gather_back)
        term[h] = lax.dot_general(
            features[...],
            proj_grad[:, cols],
            (((0,), (0,)), ((), ())),
            preferred_element_type=F32,
        )
        sum1(h)

    for h in range(H):
        source_part(h)
        if h == 0:
            row_peers(lambda q: bias1(q, q).wait_recv())
            bias_mid[...] = jnp.sum(bias_in1[...], axis=0)
            col_peers(lambda p: bias2(p, c).start())
            bias_in2[c] = bias_mid[...]
        else:
            sum3(h - 1)
        weight_part(h)
        if h > 0:
            sum4(h - 1)

    def features_back(b):
        rows = pl.ds(pl.multiple_of(b * side, side), side)
        grad_features[rows, :] = lax.dot_general(
            proj_grad[rows, :], weight[...], (((1,), (1,)), ((), ())), preferred_element_type=F32
        ).astype(BF16)

    last = H - 1
    loop(0, B // 2, features_back)
    sum2(last)
    loop(B // 2, B, features_back)
    col_peers(lambda p: bias2(p, p).wait_recv())
    grad_bias[...] = jnp.sum(jnp.sum(bias_in2[...], axis=0), axis=0, keepdims=True) * scale
    sum3(last)
    for h in range(last):
        sum5(h)
    sum4(last)
    sum5(last)
    if fuse_sum:
        for h in range(H):
            row_peers(lambda q, h=h: part1(h, q, r).wait_send())
            col_peers(lambda p, h=h: part2(h, p, c).wait_send())
            col_peers(lambda p, h=h: part3(h, p, c).wait_send())
            row_peers(lambda q, h=h: part4(h, q, r).wait_send())
    out_copy.wait()

    row_peers(
        lambda q: row_copy(
            lists.at[q], list_all.at[r], list_s.at[q], list_r.at[r], q
        ).wait_send()
    )
    row_peers(lambda q: bias1(q, r).wait_send())
    col_peers(lambda p: bias2(p, c).wait_send())
    for h in range(H):
        row_peers(lambda q, h=h: fetch_copy(h, q, r).wait_send())
        col_peers(lambda p, h=h: rows_copy(h, p, c).wait_send())
        col_peers(lambda p, h=h: slope_copy(h, p, c).wait_send())
        row_peers(lambda q, h=h: back_copy(h, q, r).wait_send())


def chain_kernel(source, target, count, prev_row, last_row, prev_src, last_src):
    tile_total = source.shape[0]
    live = count[0]
    for last in (last_row, last_src):

        def clear(s, last=last):
            last[s] = tile_total

        loop(0, last.shape[0], clear)

    def link(k):
        for slots, prev, last in ((target, prev_row, last_row), (source, prev_src, last_src)):
            slot = slots[k]
            before = last[slot]
            prev[k] = before
            last[slot] = jnp.where(k < live, k, before)

    loop(0, tile_total, link)


def body(
    features,
    weight,
    layer_bias,
    adj_tiles,
    tile_source,
    tile_target,
    tile_count,
    fetch_list,
    deliver_list,
    cotangent,
):
    R = lax.axis_size("row")
    C = lax.axis_size("col")
    H = HALVES
    N, F = features.shape
    T, side, _ = adj_tiles.shape
    B = N // side
    CF = fetch_list.shape[1]
    CO = deliver_list.shape[1]
    FC = F // H
    half = F // R
    piece = half // C
    fuse_sum = F % R == 0 and half % C == 0 and piece % 8 == 0
    scale = 1.0 / math.sqrt(N * R * C)
    list_rows = -(-CF // 8) * 8
    vmem = pl.BlockSpec(memory_space=pltpu.VMEM)
    smem = pl.BlockSpec(memory_space=pltpu.SMEM)
    hbm = pl.BlockSpec(memory_space=pl.ANY)
    prev_row, last_row, prev_src, last_src = pl.pallas_call(
        chain_kernel,
        out_shape=tuple(
            jax.ShapeDtypeStruct((size,), jnp.int32) for size in (T, C * CO, T, R * CF)
        ),
        in_specs=[smem] * 3,
        out_specs=(smem,) * 4,
    )(tile_source, tile_target, tile_count)
    V = pltpu.VMEM
    dma = pltpu.SemaphoreType.DMA
    small = piece if fuse_sum else 8
    scratch = [
        V((T, side, side), BF16),
        V((N, F), BF16),
        V((N, F), BF16),
        V((R, list_rows, F), jnp.int32),
        V((R, list_rows, F), jnp.int32),
        V((H, B, side, FC), BF16),
        V((H, R, CF, side, FC), BF16),
        V((T + 1, side, FC), F32),
        V((T, side, side), BF16),
        V((H, B, side, FC), F32),
        V((N, F), BF16),
        *[V((R, CF, side, FC), BF16)] * H,
        *[V((C, CO, side, FC), BF16)] * H,
        *[V((C, CO, side, FC), BF16)] * H,
        *[V((B, side, FC), BF16)] * H,
        *[V((C, CO, side, FC), BF16)] * H,
        *[V((C, CO, side, FC), BF16)] * H,
        *[V((R, CF, side, FC), BF16)] * H,
        *[V((R, CF, side, FC), BF16)] * H,
        V((H, F, FC), F32),
        V((8, F), F32),
        V((8, F), F32),
        V((R, 8, F), F32),
        V((8, F), F32),
        V((C, 8, F), F32),
        V((H, R, half, FC), F32),
        V((H, half, FC), F32),
        V((H, C, small, FC), F32),
        V((H, small, FC), F32),
        V((H, C, small, FC), F32),
        V((H, R, C, small, FC), F32),
        *[dma((R,))] * 2,
        *[dma((H, R))] * 2,
        *[dma((H, C))] * 2,
        *[dma((H, C))] * 2,
        *[dma((H, R))] * 2,
        *[dma((R,))] * 2,
        *[dma((C,))] * 2,
        *[dma((H, R))] * 2,
        *[dma((H, C))] * 2,
        *[dma((H, C))] * 2,
        *[dma((H, R))] * 2,
        dma((3,)),
    ]
    layer_out, grad_features, grad_weight, grad_bias = pl.pallas_call(
        functools.partial(layer_kernel, R, C, fuse_sum, scale),
        out_shape=(
            jax.ShapeDtypeStruct((N, F), BF16),
            jax.ShapeDtypeStruct((N, F), BF16),
            jax.ShapeDtypeStruct((F, F), F32),
            jax.ShapeDtypeStruct((1, F), F32),
        ),
        in_specs=[smem] * 8 + [vmem] * 3 + [hbm] * 2,
        out_specs=(hbm,) + (vmem,) * 3,
        scratch_shapes=scratch,
        compiler_params=pltpu.CompilerParams(
            collective_id=0, has_side_effects=True, vmem_limit_bytes=56 * 1024 * 1024
        ),
    )(
        tile_source,
        tile_target,
        prev_row,
        last_row,
        prev_src,
        last_src,
        fetch_list,
        deliver_list,
        features,
        weight,
        layer_bias.reshape(1, F),
        adj_tiles,
        cotangent,
    )
    grad_bias = grad_bias.reshape(F)
    if not fuse_sum:
        grad_weight = lax.psum(grad_weight, ("row", "col")) * scale
    return (layer_out, grad_features, grad_weight, grad_bias)


def solution(mesh):
    return jax.shard_map(
        body,
        mesh=mesh,
        in_specs=(
            P(("row", "col"), None),
            P(),
            P(),
            P(("row", "col"), None, None),
            P(("row", "col")),
            P(("row", "col")),
            P(("row", "col")),
            P(("row", "col"), None),
            P(("row", "col"), None),
            P(("row", "col"), None),
        ),
        out_specs=(P(("row", "col"), None), P(("row", "col"), None), P(), P()),
        check_vma=False,
    )
```

```python
import functools
import math

import jax
import jax.numpy as jnp
from jax import lax
from jax.experimental import pallas as pl
from jax.experimental.pallas import tpu as pltpu
from jax.sharding import PartitionSpec as P

F32 = jnp.float32
BF16 = jnp.bfloat16
HALVES = 2


def loop(lower, upper, step):
    def run(i, carry):
        step(i)
        return carry

    lax.fori_loop(lower, upper, run, 0)


def layer_kernel(
    R,
    C,
    scale,
    take_src,
    take_row,
    prev_row,
    last_row,
    prev_src,
    last_src,
    fetch,
    deliver,
    features,
    weight,
    bias,
    tiles_hbm,
    cotangent_hbm,
    layer_out_hbm,
    grad_features,
    grad_weight,
    grad_bias,
    *scratch,
):
    H = HALVES
    scratch = list(scratch)

    def take(count):
        taken = scratch[:count]
        del scratch[:count]
        return taken

    (tiles, cotangent, layer_out, lists, features_t) = take(5)
    (list_all, proj, fetch_out, prod, turned, agg, proj_grad) = take(7)
    src = take(H)
    rows_out = take(H)
    rows_in = take(H)
    slope = take(H)
    slope_out = take(H)
    row_vals = take(H)
    back_out = take(H)
    back_in = take(H)
    (term, bias_acc, bias_row, bias_in1, bias_mid, bias_in2) = take(6)
    (part_in, part_sum, piece_in, piece_sum, piece_all) = take(5)
    (list_s, list_r, fetch_s, fetch_r, rows_s, rows_r) = take(6)
    (slope_s, slope_r, back_s, back_r, b1_s, b1_r, b2_s, b2_r) = take(8)
    (p1_s, p1_r, p2_s, p2_r, p3_s, p3_r, local) = take(7)

    r = lax.axis_index("row")
    c = lax.axis_index("col")
    T = tiles.shape[0]
    side = tiles.shape[1]
    B = proj.shape[1]
    FC = proj.shape[3]
    CF = fetch_out.shape[2]
    CO = rows_out[0].shape[1]

    def row_copy(source, target, send, recv, q):
        return pltpu.make_async_remote_copy(
            source, target, send, recv, device_id={"row": q}, device_id_type=pl.DeviceIdType.MESH
        )

    def col_copy(source, target, send, recv, p):
        return pltpu.make_async_remote_copy(
            source, target, send, recv, device_id={"col": p}, device_id_type=pl.DeviceIdType.MESH
        )

    def row_peers(step):
        loop(1, R, lambda i: step(lax.rem(r + i, R)))

    def col_peers(step):
        loop(1, C, lambda i: step(lax.rem(c + i, C)))

    barrier = pltpu.get_barrier_semaphore()
    row_peers(
        lambda q: pl.semaphore_signal(
            barrier, inc=1, device_id={"row": q}, device_id_type=pl.DeviceIdType.MESH
        )
    )
    col_peers(
        lambda p: pl.semaphore_signal(
            barrier, inc=1, device_id={"col": p}, device_id_type=pl.DeviceIdType.MESH
        )
    )
    tiles_copy = pltpu.make_async_copy(tiles_hbm, tiles, local.at[0])
    cotangent_copy = pltpu.make_async_copy(cotangent_hbm, cotangent, local.at[1])
    out_copy = pltpu.make_async_copy(layer_out, layer_out_hbm, local.at[2])
    tiles_copy.start()
    cotangent_copy.start()
    lists[...] = jnp.full(lists.shape, -1, jnp.int32)
    for q in range(R):
        for j in range(CF):
            row = jnp.zeros((1, lists.shape[2]), jnp.int32) + fetch[q, j]
            lists[q, j : j + 1, :] = row
    pl.semaphore_wait(barrier, R + C - 2)

    row_peers(
        lambda q: row_copy(
            lists.at[q], list_all.at[r], list_s.at[q], list_r.at[r], q
        ).start()
    )
    list_all[r] = lists[r]

    def project(b):
        rows = pl.ds(pl.multiple_of(b * side, side), side)
        whole = jnp.dot(features[rows, :], weight[...], preferred_element_type=F32).astype(BF16)
        for h in range(H):
            proj[h, b] = whole[:, h * FC : (h + 1) * FC]

    loop(0, B, project)
    row_peers(
        lambda q: row_copy(
            lists.at[q], list_all.at[q], list_s.at[q], list_r.at[q], q
        ).wait_recv()
    )

    def picked(h, q, j):
        wanted = list_all[q, j : j + 1, :FC]
        total = jnp.zeros((side, FC), F32)
        for b in range(B):
            total = total + (wanted == b).astype(F32) * proj[h, b].astype(F32)
        return total.astype(BF16)

    def fetch_copy(h, q, frm):
        return row_copy(
            fetch_out.at[h, q], src[h].at[frm], fetch_s.at[h, q], fetch_r.at[h, frm], q
        )

    for h in range(H):

        def send_fetch(q, h=h):
            for j in range(CF):
                fetch_out[h, q, j] = picked(h, q, j)
            fetch_copy(h, q, r).start()

        row_peers(send_fetch)
        for j in range(CF):
            src[h][r, j] = picked(h, r, j)

    prod[T] = jnp.zeros((side, FC), F32)

    def clear(b):
        for h in range(H):
            agg[h, b] = jnp.zeros((side, FC), F32)

    loop(0, B, clear)

    group = math.gcd(T, 8)

    def tile_sums(left, right, index, cap, prev):
        def multiply(g):
            for u in range(group):
                k = g * group + u
                slot = index[k]
                prod[k] = jnp.dot(
                    left[k], right[slot // cap, lax.rem(slot, cap)], preferred_element_type=F32
                )

        loop(0, T // group, multiply)

        def chain(g):
            for u in range(group):
                k = g * group + u
                prod[k] = prod[k] + prod[prev[k]]

        loop(0, T // group, chain)

    def rows_copy(h, p, frm):
        return col_copy(
            rows_out[h].at[p], rows_in[h].at[frm], rows_s.at[h, p], rows_r.at[h, frm], p
        )

    tiles_copy.wait()
    for h in range(H):
        row_peers(lambda q, h=h: fetch_copy(h, q, q).wait_recv())
        tile_sums(tiles, src[h], take_src, CF, prev_row)

        def send_rows(p, h=h):
            for j in range(CO):
                rows_out[h][p, j] = prod[last_row[p * CO + j]].astype(BF16)
            rows_copy(h, p, c).start()

        col_peers(send_rows)
        for j in range(CO):
            rows_in[h][c, j] = prod[last_row[c * CO + j]].astype(BF16)

    def turn(g):
        for u in range(group):
            turned[g * group + u] = tiles[g * group + u].T

    loop(0, T // group, turn)

    def turn_features(b):
        rows = pl.ds(pl.multiple_of(b * side, side), side)
        features_t[:, rows] = features[rows, :].T

    loop(0, B, turn_features)

    strip = 16

    def add_rows(h, p):
        masks = [
            [(deliver[p, j] == b).astype(F32) for j in range(CO)] for b in range(B)
        ]

        def add(i):
            rows = pl.ds(pl.multiple_of(i * strip, strip), strip)
            got = [rows_in[h][p, j, rows, :].astype(F32) for j in range(CO)]
            for b in range(B):
                total = agg[h, b, rows, :]
                for j in range(CO):
                    total = total + masks[b][j] * got[j]
                agg[h, b, rows, :] = total

        loop(0, side // strip, add)

    def slope_copy(h, p, frm):
        return col_copy(
            slope_out[h].at[p], row_vals[h].at[frm], slope_s.at[h, p], slope_r.at[h, frm], p
        )

    bias_acc[...] = jnp.zeros_like(bias_acc)
    cotangent_copy.wait()
    for h in range(H):
        cols = slice(h * FC, (h + 1) * FC)
        add_rows(h, c)

        def arrive(p, h=h):
            rows_copy(h, p, p).wait_recv()
            add_rows(h, p)

        col_peers(arrive)

        def activate(b, h=h, cols=cols):
            rows = pl.ds(pl.multiple_of(b * side, side), side)
            value = agg[h, b] + bias[0:1, cols]
            logistic = 1.0 / (1.0 + jnp.exp(-value))
            layer_out[rows, cols] = (value * logistic).astype(BF16)
            grad = cotangent[rows, cols].astype(F32) * (
                logistic * (1.0 + value * (1.0 - logistic))
            )
            slope[h][b] = grad.astype(BF16)
            bias_acc[:, cols] = bias_acc[:, cols] + jnp.sum(
                grad.reshape(side // 8, 8, FC), axis=0
            )

        loop(0, B, activate)

        def send_slope(p, h=h):
            for j in range(CO):
                slope_out[h][p, j] = slope[h][jnp.maximum(deliver[p, j], 0)]
            slope_copy(h, p, c).start()

        col_peers(send_slope)
        for j in range(CO):
            row_vals[h][c, j] = slope[h][jnp.maximum(deliver[c, j], 0)]

    out_copy.start()

    bias_row[...] = bias_acc[...]

    def bias1(q, frm):
        return row_copy(bias_row, bias_in1.at[frm], b1_s.at[q], b1_r.at[frm], q)

    def bias2(p, frm):
        return col_copy(bias_mid, bias_in2.at[frm], b2_s.at[p], b2_r.at[frm], p)

    row_peers(lambda q: bias1(q, r).start())
    bias_in1[r] = bias_acc[...]

    def back_copy(h, q, frm):
        return row_copy(
            back_out[h].at[q], back_in[h].at[frm], back_s.at[h, q], back_r.at[h, frm], q
        )

    F = weight.shape[0]
    piece = F // C

    def part1(h, p, frm):
        place = pl.ds(pl.multiple_of(p * piece, 8), piece)
        return col_copy(
            term.at[h, place, :], part_in.at[h, frm], p1_s.at[h, p], p1_r.at[h, frm], p
        )

    def part2(h, q, frm):
        return row_copy(part_sum.at[h], piece_in.at[h, frm], p2_s.at[h, q], p2_r.at[h, frm], q)

    def part3(h, p, frm):
        return col_copy(piece_sum.at[h], piece_all.at[h, frm], p3_s.at[h, p], p3_r.at[h, frm], p)

    def sum1(h):
        col_peers(lambda p: part1(h, p, c).start())
        part_in[h, c] = term[h, pl.ds(pl.multiple_of(c * piece, 8), piece), :]

    def sum2(h):
        col_peers(lambda p: part1(h, p, p).wait_recv())
        part_sum[h] = jnp.sum(part_in[h], axis=0)
        row_peers(lambda q: part2(h, q, r).start())
        piece_in[h, r] = part_sum[h]

    def sum3(h):
        row_peers(lambda q: part2(h, q, q).wait_recv())
        piece_sum[h] = jnp.sum(piece_in[h], axis=0) * scale
        col_peers(lambda p: part3(h, p, c).start())
        piece_all[h, c] = piece_sum[h]

    def sum4(h):
        col_peers(lambda p: part3(h, p, p).wait_recv())
        grad_weight[:, h * FC : (h + 1) * FC] = piece_all[h].reshape(F, FC)

    def source_part(h):
        col_peers(lambda p: slope_copy(h, p, p).wait_recv())
        tile_sums(turned, row_vals[h], take_row, CO, prev_src)

        def send_back(q):
            for j in range(CF):
                back_out[h][q, j] = prod[last_src[q * CF + j]].astype(BF16)
            back_copy(h, q, r).start()

        row_peers(send_back)
        for j in range(CF):
            back_in[h][r, j] = prod[last_src[r * CF + j]].astype(BF16)

    def weight_part(h):
        cols = slice(h * FC, (h + 1) * FC)
        row_peers(lambda q: back_copy(h, q, q).wait_recv())

        def gather_back(b):
            total = jnp.zeros((side, FC), F32)
            for q in range(R):
                for j in range(CF):
                    mask = (list_all[q, j : j + 1, :FC] == b).astype(F32)
                    total = total + mask * back_in[h][q, j].astype(F32)
            rows = pl.ds(pl.multiple_of(b * side, side), side)
            proj_grad[rows, cols] = total.astype(BF16)

        loop(0, B, gather_back)
        term[h] = jnp.dot(features_t[...], proj_grad[:, cols], preferred_element_type=F32)
        sum1(h)

    for h in range(H):
        source_part(h)
        if h == 0:
            row_peers(lambda q: bias1(q, q).wait_recv())
            bias_mid[...] = jnp.sum(bias_in1[...], axis=0)
            col_peers(lambda p: bias2(p, c).start())
            bias_in2[c] = bias_mid[...]
        weight_part(h)
        if h > 0:
            sum2(h - 1)

    def features_back(b):
        rows = pl.ds(pl.multiple_of(b * side, side), side)
        grad_features[rows, :] = lax.dot_general(
            proj_grad[rows, :], weight[...], (((1,), (1,)), ((), ())), preferred_element_type=F32
        ).astype(BF16)

    last = H - 1
    loop(0, B // 2, features_back)
    for h in range(last):
        sum3(h)
    sum2(last)
    loop(B // 2, B, features_back)
    col_peers(lambda p: bias2(p, p).wait_recv())
    grad_bias[...] = jnp.sum(jnp.sum(bias_in2[...], axis=0), axis=0, keepdims=True) * scale
    sum3(last)
    for h in range(H):
        sum4(h)
        col_peers(lambda p, h=h: part1(h, p, c).wait_send())
        row_peers(lambda q, h=h: part2(h, q, r).wait_send())
        col_peers(lambda p, h=h: part3(h, p, c).wait_send())
    out_copy.wait()

    row_peers(
        lambda q: row_copy(
            lists.at[q], list_all.at[r], list_s.at[q], list_r.at[r], q
        ).wait_send()
    )
    row_peers(lambda q: bias1(q, r).wait_send())
    col_peers(lambda p: bias2(p, c).wait_send())
    for h in range(H):
        row_peers(lambda q, h=h: fetch_copy(h, q, r).wait_send())
        col_peers(lambda p, h=h: rows_copy(h, p, c).wait_send())
        col_peers(lambda p, h=h: slope_copy(h, p, c).wait_send())
        row_peers(lambda q, h=h: back_copy(h, q, r).wait_send())


def chain_kernel(source, target, count, prev_row, last_row, prev_src, last_src):
    tile_total = source.shape[0]
    live = count[0]
    for last in (last_row, last_src):

        def clear(s, last=last):
            last[s] = tile_total

        loop(0, last.shape[0], clear)

    def link(k):
        for slots, prev, last in ((target, prev_row, last_row), (source, prev_src, last_src)):
            slot = slots[k]
            before = last[slot]
            prev[k] = before
            last[slot] = jnp.where(k < live, k, before)

    loop(0, tile_total, link)


def body(
    features,
    weight,
    layer_bias,
    adj_tiles,
    tile_source,
    tile_target,
    tile_count,
    fetch_list,
    deliver_list,
    cotangent,
):
    R = lax.axis_size("row")
    C = lax.axis_size("col")
    H = HALVES
    N, F = features.shape
    T, side, _ = adj_tiles.shape
    B = N // side
    CF = fetch_list.shape[1]
    CO = deliver_list.shape[1]
    FC = F // H
    piece = F // C
    scale = 1.0 / math.sqrt(N * R * C)
    list_rows = -(-CF // 8) * 8
    vmem = pl.BlockSpec(memory_space=pltpu.VMEM)
    smem = pl.BlockSpec(memory_space=pltpu.SMEM)
    hbm = pl.BlockSpec(memory_space=pl.ANY)
    prev_row, last_row, prev_src, last_src = pl.pallas_call(
        chain_kernel,
        out_shape=tuple(
            jax.ShapeDtypeStruct((size,), jnp.int32) for size in (T, C * CO, T, R * CF)
        ),
        in_specs=[smem] * 3,
        out_specs=(smem,) * 4,
    )(tile_source, tile_target, tile_count)
    V = pltpu.VMEM
    dma = pltpu.SemaphoreType.DMA
    scratch = [
        V((T, side, side), BF16),
        V((N, F), BF16),
        V((N, F), BF16),
        V((R, list_rows, F), jnp.int32),
        V((F, N), BF16),
        V((R, list_rows, F), jnp.int32),
        V((H, B, side, FC), BF16),
        V((H, R, CF, side, FC), BF16),
        V((T + 1, side, FC), F32),
        V((T, side, side), BF16),
        V((H, B, side, FC), F32),
        V((N, F), BF16),
        *[V((R, CF, side, FC), BF16)] * H,
        *[V((C, CO, side, FC), BF16)] * H,
        *[V((C, CO, side, FC), BF16)] * H,
        *[V((B, side, FC), BF16)] * H,
        *[V((C, CO, side, FC), BF16)] * H,
        *[V((C, CO, side, FC), BF16)] * H,
        *[V((R, CF, side, FC), BF16)] * H,
        *[V((R, CF, side, FC), BF16)] * H,
        V((H, F, FC), F32),
        V((8, F), F32),
        V((8, F), F32),
        V((R, 8, F), F32),
        V((8, F), F32),
        V((C, 8, F), F32),
        V((H, C, piece, FC), F32),
        V((H, piece, FC), F32),
        V((H, R, piece, FC), F32),
        V((H, piece, FC), F32),
        V((H, C, piece, FC), F32),
        *[dma((R,))] * 2,
        *[dma((H, R))] * 2,
        *[dma((H, C))] * 2,
        *[dma((H, C))] * 2,
        *[dma((H, R))] * 2,
        *[dma((R,))] * 2,
        *[dma((C,))] * 2,
        *[dma((H, C))] * 2,
        *[dma((H, R))] * 2,
        *[dma((H, C))] * 2,
        dma((3,)),
    ]
    layer_out, grad_features, grad_weight, grad_bias = pl.pallas_call(
        functools.partial(layer_kernel, R, C, scale),
        out_shape=(
            jax.ShapeDtypeStruct((N, F), BF16),
            jax.ShapeDtypeStruct((N, F), BF16),
            jax.ShapeDtypeStruct((F, F), F32),
            jax.ShapeDtypeStruct((1, F), F32),
        ),
        in_specs=[smem] * 8 + [vmem] * 3 + [hbm] * 2,
        out_specs=(hbm,) + (vmem,) * 3,
        scratch_shapes=scratch,
        compiler_params=pltpu.CompilerParams(
            collective_id=0, has_side_effects=True, vmem_limit_bytes=56 * 1024 * 1024
        ),
    )(
        tile_source,
        tile_target,
        prev_row,
        last_row,
        prev_src,
        last_src,
        fetch_list,
        deliver_list,
        features,
        weight,
        layer_bias.reshape(1, F),
        adj_tiles,
        cotangent,
    )
    grad_bias = grad_bias.reshape(F)
    return (layer_out, grad_features, grad_weight, grad_bias)


def solution(mesh):
    return jax.shard_map(
        body,
        mesh=mesh,
        in_specs=(
            P(("row", "col"), None),
            P(),
            P(),
            P(("row", "col"), None, None),
            P(("row", "col")),
            P(("row", "col")),
            P(("row", "col")),
            P(("row", "col"), None),
            P(("row", "col"), None),
            P(("row", "col"), None),
        ),
        out_specs=(P(("row", "col"), None), P(("row", "col"), None), P(), P()),
        check_vma=False,
    )
```
